32 devices in a mesh: leaf: 8 (over z, y), col: 4 (over x, core).
Axes of the slice: x: 2, y: 2, z: 4, core: 2. Of those that a mesh axis runs over, the one named last changes fastest.
Arguments:
- child_fronts: float32 [8, 2048, 2048], P('leaf', 'col'), may hold values from -8 to 8, as said below
- child_index: int32 [8, 6], replicated, may hold values from 0 to 23, as said below
- parent_front: float32 [6144, 6144], P('leaf', 'col'), may hold values from -8 to 8, as said below
Outputs:
- child_factor: float32 [8, 2048, 512], P('leaf', 'col')
- parent_factor: float32 [6144, 6144], P('leaf', 'col')
The draws below stay inside these ranges and needn't reach their ends.
Inputs may be any that keep to these rules, and one draw needn't show every extreme that they name: `child_index`: in each row the 6 indices are distinct and so are their groups index // 3; hence one row names at most 2 indices in any aligned group of 6 blocks (blocks 6k to 6k+5), and exactly 2 in some. `child_fronts`: each child front is symmetric with diagonal entries of 0.5 to 7 and smallest eigenvalue above 0.5. `parent_front`: symmetric with diagonal entries of 0.5 to 7 and smallest eigenvalue above 0.5.
All inputs are finite; a program needn't handle non-finite values.
Results may differ from the reference program's by a relative error of at most 0.00016.
Values sent between devices are 32-bit elements; how exact they have to be, the bound alone decides.
A program may use at most 192 MiB of HBM per device.

```python
import jax
import jax.numpy as jnp
from jax import lax

B = 256
PC = 2
ROWBLK = 3
CF = 8
CC = 6
PF = 6144
CHILDREN = 8


def spd_front(key, order):
    key_factor = jax.random.fold_in(key, 0)
    key_diagonal = jax.random.fold_in(key, 2)
    factor_rank = min(order // 4, 1024)
    factor = jax.random.truncated_normal(key_factor, -4.0, 4.0, (order, factor_rank), jnp.float32)
    coupled = jnp.dot(factor, factor.T, precision=lax.Precision.HIGHEST, preferred_element_type=jnp.float32) * (1.0 / factor_rank)
    diagonal = jax.random.uniform(key_diagonal, (order,), jnp.float32, 0.5, 1.0)
    rows = lax.broadcasted_iota(jnp.int32, (order, order), 0)
    cols = lax.broadcasted_iota(jnp.int32, (order, order), 1)
    return coupled + jnp.where(rows == cols, diagonal[:, None], 0.0)


def draw_child_fronts(key, part):
    child_keys = jax.random.split(jax.random.fold_in(key, 11), CHILDREN)
    return lax.map(lambda one_key: spd_front(one_key, CF * B), child_keys)


def draw_parent_front(key, part):
    return spd_front(jax.random.fold_in(key, 13), PF)


def draw_child_index(key, part):
    base = jax.random.fold_in(key, 17)
    child_keys = jax.random.split(base, CHILDREN)
    groups = jax.vmap(lambda one_key: jax.random.permutation(one_key, CF)[:CC])(child_keys)
    offsets = jax.random.randint(jax.random.fold_in(base, 7), (CHILDREN, CC), 0, ROWBLK)
    return (groups * ROWBLK + offsets).astype(jnp.int32)


def setup_inputs(seed: int = 0) -> dict:
    arg_keys = jax.random.split(jax.random.key(seed), 4)
    return {
        "child_fronts": draw_child_fronts(jax.random.fold_in(arg_keys[3], 71), 0),
        "child_index": draw_child_index(jax.random.fold_in(arg_keys[3], 71), 0),
        "parent_front": draw_parent_front(jax.random.fold_in(arg_keys[3], 71), 0),
    }


highest = lax.Precision.HIGHEST

def partial_factor(front, width):
    pivot = jnp.linalg.cholesky(front[:width, :width])
    below = jax.scipy.linalg.solve_triangular(pivot, front[width:, :width].T, lower=True).T
    schur = front[width:, width:] - jnp.dot(below.astype(jnp.float32), below.T.astype(jnp.float32), precision=highest, preferred_element_type=jnp.float32)
    return (pivot, below, schur)

def reference(child_fronts, child_index, parent_front):
    child_width = PC * B
    offsets = jnp.arange(B, dtype=jnp.int32)
    assembled = parent_front
    factors = []
    for child in range(CHILDREN):
        pivot, below, schur = partial_factor(child_fronts[child], child_width)
        factors.append(jnp.concatenate([pivot, below], 0))
        places = (child_index[child][:, None] * B + offsets[None, :]).reshape(-1).astype(jnp.int32)
        assembled = assembled.at[places[:, None], places[None, :]].add(schur)
    width = ROWBLK * B
    pivot, below, schur = partial_factor(assembled, width)
    upper = jnp.concatenate([pivot, jnp.zeros((width, PF - width), jnp.float32)], 1)
    lower = jnp.concatenate([below, schur], 1)
    return (jnp.stack(factors), jnp.concatenate([upper, lower], 0))
```

```python
import functools

import jax
import jax.numpy as jnp
from jax import lax
from jax.experimental import pallas as pl
from jax.experimental.pallas import tpu as pltpu
from jax.sharding import PartitionSpec as P

B = 256
PC = 2
ROWBLK = 3
T = 128
W = 8

highest = lax.Precision.HIGHEST
high = lax.Precision.HIGH


def split3(x):
    h = x.astype(jnp.bfloat16)
    rest = x - h.astype(jnp.float32)
    m = rest.astype(jnp.bfloat16)
    l = (rest - m.astype(jnp.float32)).astype(jnp.bfloat16)
    return h.astype(jnp.float32), m.astype(jnp.float32), l.astype(jnp.float32)


def factor_tile(tile):
    rows = lax.broadcasted_iota(jnp.int32, (W, T), 0)
    lanes = lax.broadcasted_iota(jnp.int32, (W, T), 1)
    count = T // W
    a = [tile[W * p : W * p + W] for p in range(count)]
    v = [jnp.where(lanes == rows + W * p, 1.0, 0.0) for p in range(count)]
    for p in range(count):
        pa, pv = a[p], v[p]
        cb = [jnp.broadcast_to(pa[:, W * p + k : W * p + k + 1], (W, T)) for k in range(W)]
        for k in range(W):
            r = jnp.broadcast_to(lax.rsqrt(cb[k][k : k + 1]), (W, T))
            col = jnp.where(rows > k, cb[k] * r, 0.0)
            ra = jnp.broadcast_to(pa[k : k + 1], (W, T)) * r
            rv = jnp.broadcast_to(pv[k : k + 1], (W, T)) * r
            pa = jnp.where(rows == k, ra, pa - col * ra)
            pv = jnp.where(rows == k, rv, pv - col * rv)
            for k2 in range(k + 1, W):
                cb[k2] = cb[k2] - col * jnp.broadcast_to(col[k2 : k2 + 1], (W, T))
        a[p] = jnp.where(lanes >= rows + W * p, pa, 0.0)
        v[p] = pv
        if p < count - 1:
            both = jnp.concatenate([a[p], pv], 1)
            h, m, l = split3(both)
            left = jnp.concatenate([x[:, :T] for x in (h, h, m, h, l, m)], 0)
            right = jnp.concatenate([h, m, h, l, h, m], 0)
            delta = lax.dot_general(
                left.T.astype(jnp.bfloat16),
                right.astype(jnp.bfloat16),
                (((1,), (0,)), ((), ())),
                preferred_element_type=jnp.float32,
            )
            for q in range(p + 1, count):
                a[q] = a[q] - delta[W * q : W * q + W, :T]
                v[q] = v[q] - delta[W * q : W * q + W, T:]
    return jnp.concatenate(a, 0), jnp.concatenate(v, 0)


def mm(x, y):
    return jnp.dot(x, y, precision=highest, preferred_element_type=jnp.float32)


def mmt(x, y):
    return lax.dot_general(
        x, y, (((1,), (1,)), ((), ())), precision=highest, preferred_element_type=jnp.float32
    )


def chol_kernel(a_ref, l_ref, x_ref, work):
    n = a_ref.shape[0]
    count = n // T
    work[...] = a_ref[...]
    l_ref[...] = jnp.zeros_like(l_ref)
    x_ref[...] = jnp.zeros_like(x_ref)

    def step(j, carry):
        at = pl.ds(pl.multiple_of(j * T, T), T)
        upper, inverse = factor_tile(work[at, at])
        l_ref[at, at] = upper.T
        x_ref[at, at] = inverse
        for t in range(count):
            here = slice(t * T, t * T + T)

            @pl.when(j == t)
            def _():
                inv = x_ref[here, here]
                if t < count - 1:
                    below = slice(t * T + T, n)
                    panel = mmt(work[below, here], inv)
                    l_ref[below, here] = panel
                    for s in range(t + 1, count):
                        cut = slice(s * T, s * T + T)
                        work[s * T :, cut] = work[s * T :, cut] - mmt(
                            panel[(s - t - 1) * T :], panel[(s - t - 1) * T : (s - t) * T]
                        )
                if t > 0:
                    x_ref[here, : t * T] = -mm(inv, mm(l_ref[here, : t * T], x_ref[: t * T, : t * T]))

        return carry

    lax.fori_loop(0, count, step, 0)


def chol_inv(a):
    n = a.shape[0]
    shape = jax.ShapeDtypeStruct((n, n), jnp.float32)
    return pl.pallas_call(
        chol_kernel,
        out_shape=(shape, shape),
        in_specs=[pl.BlockSpec(memory_space=pltpu.VMEM)],
        out_specs=(pl.BlockSpec(memory_space=pltpu.VMEM),) * 2,
        scratch_shapes=[pltpu.VMEM((n, n), jnp.float32)],
        compiler_params=pltpu.CompilerParams(vmem_limit_bytes=32 * 2**20),
        cost_estimate=pl.CostEstimate(
            flops=n * 100_000_000, bytes_accessed=n * 300_000, transcendentals=n * 8
        ),
    )(a)


def place_kernel(child_count, slots, row_ref, col_ref, base_ref, piece_ref, out_ref):
    here = pl.program_id(0)
    out_ref[...] = base_ref[...]

    def body(k, carry):
        @pl.when(row_ref[k] == here)
        def _():
            for s in range(slots):
                q = col_ref[k * slots + s]

                @pl.when(q >= 0)
                def _():
                    at = pl.ds(pl.multiple_of(q * B, B), B)
                    out_ref[:, at] = out_ref[:, at] + piece_ref[k, :, s * B : s * B + B]

        return carry

    lax.fori_loop(0, child_count, body, 0)


def place(base, pieces, row_at, col_at):
    children, slots = col_at.shape
    rows, cols = base.shape
    return pl.pallas_call(
        functools.partial(place_kernel, children, slots),
        grid_spec=pltpu.PrefetchScalarGridSpec(
            num_scalar_prefetch=2,
            grid=(rows // B,),
            in_specs=[
                pl.BlockSpec((B, cols), lambda i, *_: (i, 0)),
                pl.BlockSpec(memory_space=pltpu.VMEM),
            ],
            out_specs=pl.BlockSpec((B, cols), lambda i, *_: (i, 0)),
        ),
        out_shape=jax.ShapeDtypeStruct(base.shape, jnp.float32),
        compiler_params=pltpu.CompilerParams(vmem_limit_bytes=48 * 2**20),
    )(row_at.astype(jnp.int32), col_at.reshape(-1).astype(jnp.int32), base, pieces)


def dot(x, y):
    return jnp.dot(x, y, precision=high, preferred_element_type=jnp.float32)


def find(mask):
    where = jnp.sum(
        jnp.where(mask, lax.broadcasted_iota(jnp.int32, mask.shape, mask.ndim - 1), 0), -1
    )
    return where, jnp.any(mask, -1)


def pick(array, index, size, axis, valid):
    block = lax.dynamic_slice_in_dim(array, index * size, size, axis)
    return jnp.where(valid, block, 0.0)


def route_slots(indices, col_blocks):
    target = indices // col_blocks
    count = indices.shape[-1]
    earlier_mask = lax.broadcasted_iota(jnp.int32, (count, count), 1) < lax.broadcasted_iota(
        jnp.int32, (count, count), 0
    )
    same = target[..., :, None] == target[..., None, :]
    ranking = jnp.sum((same & earlier_mask).astype(jnp.int32), axis=-1)
    return (target, ranking)


def per_device(child_fronts, child_index, parent_front):
    leaf_pos = lax.axis_index("leaf")
    col_pos = lax.axis_index("col")
    leaf_count = lax.axis_size("leaf")
    col_count = lax.axis_size("col")
    share = leaf_count // col_count
    children, contrib = child_index.shape
    front = child_fronts[0]
    row_count = front.shape[0]
    width = PC * B
    pivots = ROWBLK * B
    col_blocks = ROWBLK * leaf_count // col_count

    target, ranking = route_slots(child_index, col_blocks)
    own_index = lax.dynamic_index_in_dim(child_index, leaf_pos, 0, keepdims=False)
    own_target = lax.dynamic_index_in_dim(target, leaf_pos, 0, keepdims=False)
    own_rank = lax.dynamic_index_in_dim(ranking, leaf_pos, 0, keepdims=False)
    own_slot = own_target * share + own_rank
    slot_block, slot_valid = find(jnp.arange(col_count * share)[:, None] == own_slot[None])
    leaf_block, leaf_valid = find(jnp.arange(leaf_count)[:, None] == (own_index // ROWBLK)[None])
    zero_block, zero_valid = leaf_block[0], leaf_valid[0]

    panel = lax.all_gather(front[:, :width], "col", axis=0, tiled=True)
    trailing = front[:, width:]
    pivot_cols = lax.all_gather(
        pick(trailing, zero_block, B, 1, zero_valid), "col", axis=0, tiled=True
    )
    outgoing = jnp.concatenate(
        [pick(trailing, slot_block[i], B, 1, slot_valid[i])[None] for i in range(col_count * share)],
        0,
    ).reshape(col_count, share, row_count, B)
    raw_cols = lax.all_to_all(outgoing, "col", split_axis=0, concat_axis=0, tiled=True)

    first_leaf, first_col = leaf_pos == 0, col_pos == 0
    root = first_leaf & first_col
    corner = parent_front[:, :pivots]
    base_pivot = lax.psum(jnp.where(root, corner, 0.0), ("leaf", "col"))
    base_rows = lax.psum(jnp.where(first_col, corner, 0.0), "col")
    base_cols = lax.psum(jnp.where(first_leaf, parent_front, 0.0), "leaf")

    factor, inverse = chol_inv(panel[:width])
    solved = dot(panel, inverse.T)
    own_rows = lax.dynamic_slice_in_dim(solved, col_pos * row_count, row_count, 0)
    child_out = jnp.where(first_col, factor, own_rows)[None]
    below = solved[width:]

    first_slot = col_pos * share
    chosen = []
    for s in range(share):
        chosen.append(
            pick(
                below,
                lax.dynamic_index_in_dim(slot_block, first_slot + s, 0, keepdims=False),
                B,
                0,
                lax.dynamic_index_in_dim(slot_valid, first_slot + s, 0, keepdims=False),
            )
        )
    zero_rows = pick(below, zero_block, B, 0, zero_valid)

    pivot_schur = pivot_cols[width:] - dot(below, zero_rows.T)
    middle = pick(pivot_schur, zero_block, B, 0, zero_valid)
    diagonal = lax.all_gather(middle, "leaf", axis=0, tiled=False)

    crossing = jnp.concatenate(
        [
            pick(
                pivot_schur,
                lax.dynamic_index_in_dim(slot_block, first_slot + s, 0, keepdims=False),
                B,
                0,
                lax.dynamic_index_in_dim(slot_valid, first_slot + s, 0, keepdims=False),
            ).T
            for s in range(share)
        ],
        1,
    )
    crossing = lax.all_gather(crossing, "leaf", axis=0, tiled=False)

    raw = raw_cols.transpose(0, 2, 1, 3).reshape(col_count * row_count, share * B)[width:]
    schur_cols = raw - dot(below, jnp.concatenate(chosen, 0).T)
    sent = jnp.concatenate([schur_cols, pivot_schur], 1)
    outgoing_rows = jnp.concatenate(
        [pick(sent, leaf_block[i], B, 0, leaf_valid[i])[None] for i in range(leaf_count)], 0
    )
    arrived = lax.all_to_all(outgoing_rows, "leaf", split_axis=0, concat_axis=0, tiled=True)

    in_zero = child_index // ROWBLK == 0
    zero_any = jnp.any(in_zero, -1)
    zero_at = jnp.where(zero_any, jnp.sum(jnp.where(in_zero, child_index % ROWBLK, 0), -1), -1)
    parts = []
    for i in range(ROWBLK):
        here = base_pivot[i * B : i * B + B]
        added = jnp.sum(jnp.where((zero_at == i)[:, None, None], diagonal, 0.0), 0)
        parts.append(
            jnp.concatenate(
                [
                    here[:, j * B : j * B + B] + (added if i == j else 0.0)
                    for j in range(ROWBLK)
                ],
                1,
            )
        )
    parent_pivot, parent_inverse = chol_inv(jnp.concatenate(parts, 0))

    in_row = child_index // ROWBLK == leaf_pos
    row_block, row_valid = find(in_row)
    row_at = jnp.where(
        row_valid, jnp.sum(jnp.where(in_row, child_index % ROWBLK, 0), -1), -1
    )
    col_at = []
    for s in range(share):
        hit = (target == col_pos) & (ranking == s)
        col_at.append(
            jnp.where(
                jnp.any(hit, -1),
                jnp.sum(jnp.where(hit, child_index - col_pos * col_blocks, 0), -1),
                -1,
            )
        )
    col_at = jnp.stack(col_at, 1)

    own_cols = col_blocks
    joined = jnp.concatenate([parent_front, base_rows], 1)
    joined_at = jnp.concatenate(
        [col_at, jnp.where(zero_at >= 0, zero_at + own_cols, -1)[:, None]], 1
    )
    joined = place(joined, arrived, row_at, joined_at)
    assembled, raw_rows = joined[:, : own_cols * B], joined[:, own_cols * B :]
    raw_top = place(base_cols, crossing, zero_at, col_at)
    row_panel = dot(raw_rows, parent_inverse.T)
    top = dot(parent_inverse, raw_top)
    schur = assembled - dot(row_panel, top)
    left = jnp.where(first_leaf, parent_pivot, row_panel)
    right = jnp.where(first_leaf, 0.0, schur[:, pivots:])
    left = jnp.where(first_col, left, jnp.where(first_leaf, 0.0, schur[:, :pivots]))
    return (child_out, jnp.concatenate([left, right], 1))


def solution(mesh):
    placed = (P("leaf", "col", None), P(), P("leaf", "col"))
    return jax.shard_map(
        per_device,
        mesh=mesh,
        in_specs=placed,
        out_specs=(P("leaf", "col", None), P("leaf", "col")),
        check_vma=False,
    )
```

```python
import functools

import jax
import jax.numpy as jnp
from jax import lax
from jax.experimental import pallas as pl
from jax.experimental.pallas import tpu as pltpu
from jax.sharding import PartitionSpec as P

B = 256
PC = 2
ROWBLK = 3
T = 128
W = 8

highest = lax.Precision.HIGHEST
high = lax.Precision.HIGH


def split3(x):
    h = x.astype(jnp.bfloat16)
    rest = x - h.astype(jnp.float32)
    m = rest.astype(jnp.bfloat16)
    l = (rest - m.astype(jnp.float32)).astype(jnp.bfloat16)
    return h.astype(jnp.float32), m.astype(jnp.float32), l.astype(jnp.float32)


def factor_tile(tile):
    rows = lax.broadcasted_iota(jnp.int32, (W, T), 0)
    lanes = lax.broadcasted_iota(jnp.int32, (W, T), 1)
    count = T // W
    a = [tile[W * p : W * p + W] for p in range(count)]
    v = [jnp.where(lanes == rows + W * p, 1.0, 0.0) for p in range(count)]
    for p in range(count):
        pa, pv = a[p], v[p]
        cb = [jnp.broadcast_to(pa[:, W * p + k : W * p + k + 1], (W, T)) for k in range(W)]
        for k in range(W):
            r = jnp.broadcast_to(lax.rsqrt(cb[k][k : k + 1]), (W, T))
            col = jnp.where(rows > k, cb[k] * r, 0.0)
            ra = jnp.broadcast_to(pa[k : k + 1], (W, T)) * r
            rv = jnp.broadcast_to(pv[k : k + 1], (W, T)) * r
            pa = jnp.where(rows == k, ra, pa - col * ra)
            pv = jnp.where(rows == k, rv, pv - col * rv)
            for k2 in range(k + 1, W):
                cb[k2] = cb[k2] - col * jnp.broadcast_to(col[k2 : k2 + 1], (W, T))
        a[p] = jnp.where(lanes >= rows + W * p, pa, 0.0)
        v[p] = pv
        if p < count - 1:
            both = jnp.concatenate([a[p], pv], 1)
            h, m, l = split3(both)
            left = jnp.concatenate([x[:, :T] for x in (h, h, m, h, l, m)], 0)
            right = jnp.concatenate([h, m, h, l, h, m], 0)
            delta = lax.dot_general(
                left.T.astype(jnp.bfloat16),
                right.astype(jnp.bfloat16),
                (((1,), (0,)), ((), ())),
                preferred_element_type=jnp.float32,
            )
            for q in range(p + 1, count):
                a[q] = a[q] - delta[W * q : W * q + W, :T]
                v[q] = v[q] - delta[W * q : W * q + W, T:]
    return jnp.concatenate(a, 0), jnp.concatenate(v, 0)


def mm(x, y):
    return jnp.dot(x, y, precision=highest, preferred_element_type=jnp.float32)


def mmt(x, y):
    return lax.dot_general(
        x, y, (((1,), (1,)), ((), ())), precision=highest, preferred_element_type=jnp.float32
    )


def chol_kernel(a_ref, l_ref, x_ref, work):
    n = a_ref.shape[0]
    count = n // T
    work[...] = a_ref[...]
    l_ref[...] = jnp.zeros_like(l_ref)
    x_ref[...] = jnp.zeros_like(x_ref)

    def step(j, carry):
        at = pl.ds(pl.multiple_of(j * T, T), T)
        upper, inverse = factor_tile(work[at, at])
        l_ref[at, at] = upper.T
        x_ref[at, at] = inverse
        for t in range(count):
            here = slice(t * T, t * T + T)

            @pl.when(j == t)
            def _():
                inv = x_ref[here, here]
                if t < count - 1:
                    below = slice(t * T + T, n)
                    panel = mmt(work[below, here], inv)
                    l_ref[below, here] = panel
                    for s in range(t + 1, count):
                        cut = slice(s * T, s * T + T)
                        work[s * T :, cut] = work[s * T :, cut] - mmt(
                            panel[(s - t - 1) * T :], panel[(s - t - 1) * T : (s - t) * T]
                        )
                if t > 0:
                    x_ref[here, : t * T] = -mm(inv, mm(l_ref[here, : t * T], x_ref[: t * T, : t * T]))

        return carry

    lax.fori_loop(0, count, step, 0)


def chol_inv(a):
    n = a.shape[0]
    shape = jax.ShapeDtypeStruct((n, n), jnp.float32)
    return pl.pallas_call(
        chol_kernel,
        out_shape=(shape, shape),
        in_specs=[pl.BlockSpec(memory_space=pltpu.VMEM)],
        out_specs=(pl.BlockSpec(memory_space=pltpu.VMEM),) * 2,
        scratch_shapes=[pltpu.VMEM((n, n), jnp.float32)],
        compiler_params=pltpu.CompilerParams(vmem_limit_bytes=32 * 2**20),
        cost_estimate=pl.CostEstimate(
            flops=n * 100_000_000, bytes_accessed=n * 300_000, transcendentals=n * 8
        ),
    )(a)


def place_kernel(child_count, slots, row_ref, col_ref, base_ref, piece_ref, out_ref):
    here = pl.program_id(0)
    out_ref[...] = base_ref[...]

    def body(k, carry):
        @pl.when(row_ref[k] == here)
        def _():
            for s in range(slots):
                q = col_ref[k * slots + s]

                @pl.when(q >= 0)
                def _():
                    at = pl.ds(pl.multiple_of(q * B, B), B)
                    out_ref[:, at] = out_ref[:, at] + piece_ref[k, :, s * B : s * B + B]

        return carry

    lax.fori_loop(0, child_count, body, 0)


def place(base, pieces, row_at, col_at):
    children, slots = col_at.shape
    rows, cols = base.shape
    return pl.pallas_call(
        functools.partial(place_kernel, children, slots),
        grid_spec=pltpu.PrefetchScalarGridSpec(
            num_scalar_prefetch=2,
            grid=(rows // B,),
            in_specs=[
                pl.BlockSpec((B, cols), lambda i, *_: (i, 0)),
                pl.BlockSpec(memory_space=pltpu.VMEM),
            ],
            out_specs=pl.BlockSpec((B, cols), lambda i, *_: (i, 0)),
        ),
        out_shape=jax.ShapeDtypeStruct(base.shape, jnp.float32),
        compiler_params=pltpu.CompilerParams(vmem_limit_bytes=48 * 2**20),
    )(row_at.astype(jnp.int32), col_at.reshape(-1).astype(jnp.int32), base, pieces)


def dot(x, y):
    return jnp.dot(x, y, precision=high, preferred_element_type=jnp.float32)


def find(mask):
    where = jnp.sum(
        jnp.where(mask, lax.broadcasted_iota(jnp.int32, mask.shape, mask.ndim - 1), 0), -1
    )
    return where, jnp.any(mask, -1)


def pick(array, index, size, axis, valid):
    block = lax.dynamic_slice_in_dim(array, index * size, size, axis)
    return jnp.where(valid, block, 0.0)


def route_slots(indices, col_blocks):
    target = indices // col_blocks
    count = indices.shape[-1]
    earlier_mask = lax.broadcasted_iota(jnp.int32, (count, count), 1) < lax.broadcasted_iota(
        jnp.int32, (count, count), 0
    )
    same = target[..., :, None] == target[..., None, :]
    ranking = jnp.sum((same & earlier_mask).astype(jnp.int32), axis=-1)
    return (target, ranking)


def per_device(child_fronts, child_index, parent_front):
    leaf_pos = lax.axis_index("leaf")
    col_pos = lax.axis_index("col")
    leaf_count = lax.axis_size("leaf")
    col_count = lax.axis_size("col")
    share = leaf_count // col_count
    children, contrib = child_index.shape
    front = child_fronts[0]
    row_count = front.shape[0]
    width = PC * B
    pivots = ROWBLK * B
    col_blocks = ROWBLK * leaf_count // col_count

    target, ranking = route_slots(child_index, col_blocks)
    own_index = lax.dynamic_index_in_dim(child_index, leaf_pos, 0, keepdims=False)
    own_target = lax.dynamic_index_in_dim(target, leaf_pos, 0, keepdims=False)
    own_rank = lax.dynamic_index_in_dim(ranking, leaf_pos, 0, keepdims=False)
    own_slot = own_target * share + own_rank
    slot_block, slot_valid = find(jnp.arange(col_count * share)[:, None] == own_slot[None])
    leaf_block, leaf_valid = find(jnp.arange(leaf_count)[:, None] == (own_index // ROWBLK)[None])
    zero_block, zero_valid = leaf_block[0], leaf_valid[0]

    panel = lax.all_gather(front[:, :width], "col", axis=0, tiled=True)
    trailing = front[:, width:]
    pivot_cols = lax.all_gather(
        pick(trailing, zero_block, B, 1, zero_valid), "col", axis=0, tiled=True
    )
    outgoing = jnp.concatenate(
        [pick(trailing, slot_block[i], B, 1, slot_valid[i])[None] for i in range(col_count * share)],
        0,
    ).reshape(col_count, share, row_count, B)
    first_leaf, first_col = leaf_pos == 0, col_pos == 0
    corner = parent_front[:, :pivots]
    part = pivots // col_count
    quarter = jnp.where(first_col, corner[:part], 0.0)
    for d in range(1, col_count):
        quarter = quarter + lax.ppermute(corner[d * part : d * part + part], "col", [(0, d)])
    quarter, panel, outgoing = lax.optimization_barrier((quarter, panel, outgoing))
    quarter = lax.psum(jnp.where(first_leaf, quarter, 0.0), "leaf")
    front_cols = jnp.where(first_leaf, parent_front, 0.0)
    raw_cols = lax.all_to_all(outgoing, "col", split_axis=0, concat_axis=0, tiled=True)
    factor, inverse = chol_inv(panel[:width])
    factor, inverse, raw_cols, corner, quarter, front_cols = lax.optimization_barrier(
        (factor, inverse, raw_cols, corner, quarter, front_cols)
    )
    base_pivot = lax.all_gather(quarter, "col", axis=0, tiled=True)
    base_cols = lax.psum(front_cols, "leaf")
    base_rows = jnp.where(first_col, corner, 0.0)
    for d in range(1, col_count):
        base_rows = base_rows + lax.ppermute(corner, "col", [(0, d)])
    solved = dot(panel, inverse.T)
    own_rows = lax.dynamic_slice_in_dim(solved, col_pos * row_count, row_count, 0)
    child_out = jnp.where(first_col, factor, own_rows)[None]
    below = solved[width:]

    first_slot = col_pos * share
    chosen = []
    for s in range(share):
        chosen.append(
            pick(
                below,
                lax.dynamic_index_in_dim(slot_block, first_slot + s, 0, keepdims=False),
                B,
                0,
                lax.dynamic_index_in_dim(slot_valid, first_slot + s, 0, keepdims=False),
            )
        )
    zero_rows = pick(below, zero_block, B, 0, zero_valid)

    pivot_schur = pivot_cols[width:] - dot(below, zero_rows.T)
    middle = pick(pivot_schur, zero_block, B, 0, zero_valid)
    diagonal = lax.all_gather(middle, "leaf", axis=0, tiled=False)

    crossing = jnp.concatenate(
        [
            pick(
                pivot_schur,
                lax.dynamic_index_in_dim(slot_block, first_slot + s, 0, keepdims=False),
                B,
                0,
                lax.dynamic_index_in_dim(slot_valid, first_slot + s, 0, keepdims=False),
            ).T
            for s in range(share)
        ],
        1,
    )
    crossing = lax.all_gather(crossing, "leaf", axis=0, tiled=False)

    raw = raw_cols.transpose(0, 2, 1, 3).reshape(col_count * row_count, share * B)[width:]
    schur_cols = raw - dot(below, jnp.concatenate(chosen, 0).T)
    sent = jnp.concatenate([schur_cols, pivot_schur], 1)
    outgoing_rows = jnp.concatenate(
        [pick(sent, leaf_block[i], B, 0, leaf_valid[i])[None] for i in range(leaf_count)], 0
    )
    arrived = lax.all_to_all(outgoing_rows, "leaf", split_axis=0, concat_axis=0, tiled=True)

    in_zero = child_index // ROWBLK == 0
    zero_any = jnp.any(in_zero, -1)
    zero_at = jnp.where(zero_any, jnp.sum(jnp.where(in_zero, child_index % ROWBLK, 0), -1), -1)
    parts = []
    for i in range(ROWBLK):
        here = base_pivot[i * B : i * B + B]
        added = jnp.sum(jnp.where((zero_at == i)[:, None, None], diagonal, 0.0), 0)
        parts.append(
            jnp.concatenate(
                [
                    here[:, j * B : j * B + B] + (added if i == j else 0.0)
                    for j in range(ROWBLK)
                ],
                1,
            )
        )
    parent_pivot, parent_inverse = chol_inv(jnp.concatenate(parts, 0))

    in_row = child_index // ROWBLK == leaf_pos
    row_block, row_valid = find(in_row)
    row_at = jnp.where(
        row_valid, jnp.sum(jnp.where(in_row, child_index % ROWBLK, 0), -1), -1
    )
    col_at = []
    for s in range(share):
        hit = (target == col_pos) & (ranking == s)
        col_at.append(
            jnp.where(
                jnp.any(hit, -1),
                jnp.sum(jnp.where(hit, child_index - col_pos * col_blocks, 0), -1),
                -1,
            )
        )
    col_at = jnp.stack(col_at, 1)

    own_cols = col_blocks
    joined = jnp.concatenate([parent_front, base_rows], 1)
    joined_at = jnp.concatenate(
        [col_at, jnp.where(zero_at >= 0, zero_at + own_cols, -1)[:, None]], 1
    )
    joined = place(joined, arrived, row_at, joined_at)
    assembled, raw_rows = joined[:, : own_cols * B], joined[:, own_cols * B :]
    raw_top = place(base_cols, crossing, zero_at, col_at)
    row_panel = dot(raw_rows, parent_inverse.T)
    top = dot(parent_inverse, raw_top)
    schur = assembled - dot(row_panel, top)
    left = jnp.where(first_leaf, parent_pivot, row_panel)
    right = jnp.where(first_leaf, 0.0, schur[:, pivots:])
    left = jnp.where(first_col, left, jnp.where(first_leaf, 0.0, schur[:, :pivots]))
    return (child_out, jnp.concatenate([left, right], 1))


def solution(mesh):
    placed = (P("leaf", "col", None), P(), P("leaf", "col"))
    return jax.shard_map(
        per_device,
        mesh=mesh,
        in_specs=placed,
        out_specs=(P("leaf", "col", None), P("leaf", "col")),
        check_vma=False,
    )
```

```python
import functools

import jax
import jax.numpy as jnp
from jax import lax
from jax.experimental import pallas as pl
from jax.experimental.pallas import tpu as pltpu
from jax.sharding import PartitionSpec as P

B = 256
PC = 2
ROWBLK = 3
T = 128
W = 8

highest = lax.Precision.HIGHEST
high = lax.Precision.HIGH


def split3(x):
    h = x.astype(jnp.bfloat16)
    rest = x - h.astype(jnp.float32)
    m = rest.astype(jnp.bfloat16)
    l = (rest - m.astype(jnp.float32)).astype(jnp.bfloat16)
    return h.astype(jnp.float32), m.astype(jnp.float32), l.astype(jnp.float32)


def factor_tile(tile):
    rows = lax.broadcasted_iota(jnp.int32, (W, T), 0)
    lanes = lax.broadcasted_iota(jnp.int32, (W, T), 1)
    count = T // W
    a = [tile[W * p : W * p + W] for p in range(count)]
    v = [jnp.where(lanes == rows + W * p, 1.0, 0.0) for p in range(count)]
    for p in range(count):
        pa, pv = a[p], v[p]
        cb = [jnp.broadcast_to(pa[:, W * p + k : W * p + k + 1], (W, T)) for k in range(W)]
        for k in range(W):
            r = jnp.broadcast_to(lax.rsqrt(cb[k][k : k + 1]), (W, T))
            col = jnp.where(rows > k, cb[k] * r, 0.0)
            ra = jnp.broadcast_to(pa[k : k + 1], (W, T)) * r
            rv = jnp.broadcast_to(pv[k : k + 1], (W, T)) * r
            pa = jnp.where(rows == k, ra, pa - col * ra)
            pv = jnp.where(rows == k, rv, pv - col * rv)
            for k2 in range(k + 1, W):
                cb[k2] = cb[k2] - col * jnp.broadcast_to(col[k2 : k2 + 1], (W, T))
        a[p] = jnp.where(lanes >= rows + W * p, pa, 0.0)
        v[p] = pv
        if p < count - 1:
            both = jnp.concatenate([a[p], pv], 1)
            h, m, l = split3(both)
            left = jnp.concatenate([x[:, :T] for x in (h, h, m, h, l, m)], 0)
            right = jnp.concatenate([h, m, h, l, h, m], 0)
            delta = lax.dot_general(
                left.T.astype(jnp.bfloat16),
                right.astype(jnp.bfloat16),
                (((1,), (0,)), ((), ())),
                preferred_element_type=jnp.float32,
            )
            for q in range(p + 1, count):
                a[q] = a[q] - delta[W * q : W * q + W, :T]
                v[q] = v[q] - delta[W * q : W * q + W, T:]
    return jnp.concatenate(a, 0), jnp.concatenate(v, 0)


def mm(x, y):
    return jnp.dot(x, y, precision=highest, preferred_element_type=jnp.float32)


def mmt(x, y):
    return lax.dot_general(
        x, y, (((1,), (1,)), ((), ())), precision=highest, preferred_element_type=jnp.float32
    )


def chol_kernel(a_ref, l_ref, x_ref, work):
    n = a_ref.shape[0]
    count = n // T
    work[...] = a_ref[...]
    l_ref[...] = jnp.zeros_like(l_ref)
    x_ref[...] = jnp.zeros_like(x_ref)

    def step(j, carry):
        at = pl.ds(pl.multiple_of(j * T, T), T)
        upper, inverse = factor_tile(work[at, at])
        l_ref[at, at] = upper.T
        x_ref[at, at] = inverse
        for t in range(count):
            here = slice(t * T, t * T + T)

            @pl.when(j == t)
            def _():
                inv = x_ref[here, here]
                if t < count - 1:
                    below = slice(t * T + T, n)
                    panel = mmt(work[below, here], inv)
                    l_ref[below, here] = panel
                    for s in range(t + 1, count):
                        cut = slice(s * T, s * T + T)
                        work[s * T :, cut] = work[s * T :, cut] - mmt(
                            panel[(s - t - 1) * T :], panel[(s - t - 1) * T : (s - t) * T]
                        )
                if t > 0:
                    x_ref[here, : t * T] = -mm(inv, mm(l_ref[here, : t * T], x_ref[: t * T, : t * T]))

        return carry

    lax.fori_loop(0, count, step, 0)


def chol_inv(a):
    n = a.shape[0]
    shape = jax.ShapeDtypeStruct((n, n), jnp.float32)
    return pl.pallas_call(
        chol_kernel,
        out_shape=(shape, shape),
        in_specs=[pl.BlockSpec(memory_space=pltpu.VMEM)],
        out_specs=(pl.BlockSpec(memory_space=pltpu.VMEM),) * 2,
        scratch_shapes=[pltpu.VMEM((n, n), jnp.float32)],
        compiler_params=pltpu.CompilerParams(vmem_limit_bytes=32 * 2**20),
        cost_estimate=pl.CostEstimate(
            flops=n * 100_000_000, bytes_accessed=n * 300_000, transcendentals=n * 8
        ),
    )(a)


def place_kernel(child_count, slots, row_ref, col_ref, base_ref, piece_ref, out_ref):
    here = pl.program_id(0)
    out_ref[...] = base_ref[...]

    def body(k, carry):
        @pl.when(row_ref[k] == here)
        def _():
            for s in range(slots):
                q = col_ref[k * slots + s]

                @pl.when(q >= 0)
                def _():
                    at = pl.ds(pl.multiple_of(q * B, B), B)
                    out_ref[:, at] = out_ref[:, at] + piece_ref[k, :, s * B : s * B + B]

        return carry

    lax.fori_loop(0, child_count, body, 0)


def place(base, pieces, row_at, col_at):
    children, slots = col_at.shape
    rows, cols = base.shape
    return pl.pallas_call(
        functools.partial(place_kernel, children, slots),
        grid_spec=pltpu.PrefetchScalarGridSpec(
            num_scalar_prefetch=2,
            grid=(rows // B,),
            in_specs=[
                pl.BlockSpec((B, cols), lambda i, *_: (i, 0)),
                pl.BlockSpec(memory_space=pltpu.VMEM),
            ],
            out_specs=pl.BlockSpec((B, cols), lambda i, *_: (i, 0)),
        ),
        out_shape=jax.ShapeDtypeStruct(base.shape, jnp.float32),
        compiler_params=pltpu.CompilerParams(vmem_limit_bytes=48 * 2**20),
    )(row_at.astype(jnp.int32), col_at.reshape(-1).astype(jnp.int32), base, pieces)


def dot(x, y):
    return jnp.dot(x, y, precision=high, preferred_element_type=jnp.float32)


def find(mask):
    where = jnp.sum(
        jnp.where(mask, lax.broadcasted_iota(jnp.int32, mask.shape, mask.ndim - 1), 0), -1
    )
    return where, jnp.any(mask, -1)


def pick(array, index, size, axis, valid):
    block = lax.dynamic_slice_in_dim(array, index * size, size, axis)
    return jnp.where(valid, block, 0.0)


def route_slots(indices, col_blocks):
    target = indices // col_blocks
    count = indices.shape[-1]
    earlier_mask = lax.broadcasted_iota(jnp.int32, (count, count), 1) < lax.broadcasted_iota(
        jnp.int32, (count, count), 0
    )
    same = target[..., :, None] == target[..., None, :]
    ranking = jnp.sum((same & earlier_mask).astype(jnp.int32), axis=-1)
    return (target, ranking)


def per_device(child_fronts, child_index, parent_front):
    leaf_pos = lax.axis_index("leaf")
    col_pos = lax.axis_index("col")
    leaf_count = lax.axis_size("leaf")
    col_count = lax.axis_size("col")
    share = leaf_count // col_count
    children, contrib = child_index.shape
    front = child_fronts[0]
    row_count = front.shape[0]
    width = PC * B
    pivots = ROWBLK * B
    col_blocks = ROWBLK * leaf_count // col_count

    target, ranking = route_slots(child_index, col_blocks)
    own_index = lax.dynamic_index_in_dim(child_index, leaf_pos, 0, keepdims=False)
    own_target = lax.dynamic_index_in_dim(target, leaf_pos, 0, keepdims=False)
    own_rank = lax.dynamic_index_in_dim(ranking, leaf_pos, 0, keepdims=False)
    own_slot = own_target * share + own_rank
    slot_block, slot_valid = find(jnp.arange(col_count * share)[:, None] == own_slot[None])
    leaf_block, leaf_valid = find(jnp.arange(leaf_count)[:, None] == (own_index // ROWBLK)[None])
    zero_block, zero_valid = leaf_block[0], leaf_valid[0]

    panel = lax.all_gather(front[:, :width], "col", axis=0, tiled=True)
    trailing = front[:, width:]
    pivot_cols = lax.all_gather(
        pick(trailing, zero_block, B, 1, zero_valid), "col", axis=0, tiled=True
    )
    outgoing = jnp.concatenate(
        [pick(trailing, slot_block[i], B, 1, slot_valid[i])[None] for i in range(col_count * share)],
        0,
    ).reshape(col_count, share, row_count, B)
    first_leaf, first_col = leaf_pos == 0, col_pos == 0
    corner = parent_front[:, :pivots]
    part = pivots // col_count
    quarter = jnp.where(first_col, corner[:part], 0.0)
    for d in range(1, col_count):
        quarter = quarter + lax.ppermute(corner[d * part : d * part + part], "col", [(0, d)])
    quarter, panel, outgoing = lax.optimization_barrier((quarter, panel, outgoing))
    front_cols = jnp.where(first_leaf, parent_front, 0.0)
    raw_cols = lax.all_to_all(outgoing, "col", split_axis=0, concat_axis=0, tiled=True)
    factor, inverse = chol_inv(panel[:width])
    factor, inverse, raw_cols, corner, quarter, front_cols = lax.optimization_barrier(
        (factor, inverse, raw_cols, corner, quarter, front_cols)
    )
    quarter = lax.psum(jnp.where(first_leaf, quarter, 0.0), "leaf")
    base_pivot = lax.all_gather(quarter, "col", axis=0, tiled=True)
    base_rows = jnp.where(first_col, corner, 0.0)
    for d in range(1, col_count):
        base_rows = base_rows + lax.ppermute(corner, "col", [(0, d)])
    solved = dot(panel, inverse.T)
    own_rows = lax.dynamic_slice_in_dim(solved, col_pos * row_count, row_count, 0)
    child_out = jnp.where(first_col, factor, own_rows)[None]
    below = solved[width:]

    first_slot = col_pos * share
    chosen = []
    for s in range(share):
        chosen.append(
            pick(
                below,
                lax.dynamic_index_in_dim(slot_block, first_slot + s, 0, keepdims=False),
                B,
                0,
                lax.dynamic_index_in_dim(slot_valid, first_slot + s, 0, keepdims=False),
            )
        )
    zero_rows = pick(below, zero_block, B, 0, zero_valid)

    pivot_schur = pivot_cols[width:] - dot(below, zero_rows.T)
    middle = pick(pivot_schur, zero_block, B, 0, zero_valid)
    diagonal = lax.all_gather(middle, "leaf", axis=0, tiled=False)

    crossing = jnp.concatenate(
        [
            pick(
                pivot_schur,
                lax.dynamic_index_in_dim(slot_block, first_slot + s, 0, keepdims=False),
                B,
                0,
                lax.dynamic_index_in_dim(slot_valid, first_slot + s, 0, keepdims=False),
            ).T
            for s in range(share)
        ],
        1,
    )
    in_zero = child_index // ROWBLK == 0
    zero_any = jnp.any(in_zero, -1)
    zero_at = jnp.where(zero_any, jnp.sum(jnp.where(in_zero, child_index % ROWBLK, 0), -1), -1)
    col_at = []
    for s in range(share):
        hit = (target == col_pos) & (ranking == s)
        col_at.append(
            jnp.where(
                jnp.any(hit, -1),
                jnp.sum(jnp.where(hit, child_index - col_pos * col_blocks, 0), -1),
                -1,
            )
        )
    col_at = jnp.stack(col_at, 1)

    raw_top = place(
        front_cols,
        crossing[None],
        lax.dynamic_slice_in_dim(zero_at, leaf_pos, 1, 0),
        lax.dynamic_slice_in_dim(col_at, leaf_pos, 1, 0),
    )
    raw_top, base_pivot = lax.optimization_barrier((raw_top, base_pivot))
    raw_top = lax.psum(raw_top, "leaf")

    raw = raw_cols.transpose(0, 2, 1, 3).reshape(col_count * row_count, share * B)[width:]
    schur_cols = raw - dot(below, jnp.concatenate(chosen, 0).T)
    sent = jnp.concatenate([schur_cols, pivot_schur], 1)
    outgoing_rows = jnp.concatenate(
        [pick(sent, leaf_block[i], B, 0, leaf_valid[i])[None] for i in range(leaf_count)], 0
    )
    arrived = lax.all_to_all(outgoing_rows, "leaf", split_axis=0, concat_axis=0, tiled=True)

    parts = []
    for i in range(ROWBLK):
        here = base_pivot[i * B : i * B + B]
        added = jnp.sum(jnp.where((zero_at == i)[:, None, None], diagonal, 0.0), 0)
        parts.append(
            jnp.concatenate(
                [
                    here[:, j * B : j * B + B] + (added if i == j else 0.0)
                    for j in range(ROWBLK)
                ],
                1,
            )
        )
    parent_pivot, parent_inverse = chol_inv(jnp.concatenate(parts, 0))

    in_row = child_index // ROWBLK == leaf_pos
    row_block, row_valid = find(in_row)
    row_at = jnp.where(
        row_valid, jnp.sum(jnp.where(in_row, child_index % ROWBLK, 0), -1), -1
    )
    own_cols = col_blocks
    joined = jnp.concatenate([parent_front, base_rows], 1)
    joined_at = jnp.concatenate(
        [col_at, jnp.where(zero_at >= 0, zero_at + own_cols, -1)[:, None]], 1
    )
    joined = place(joined, arrived, row_at, joined_at)
    assembled, raw_rows = joined[:, : own_cols * B], joined[:, own_cols * B :]
    row_panel = dot(raw_rows, parent_inverse.T)
    top = dot(parent_inverse, raw_top)
    schur = assembled - dot(row_panel, top)
    left = jnp.where(first_leaf, parent_pivot, row_panel)
    right = jnp.where(first_leaf, 0.0, schur[:, pivots:])
    left = jnp.where(first_col, left, jnp.where(first_leaf, 0.0, schur[:, :pivots]))
    return (child_out, jnp.concatenate([left, right], 1))


def solution(mesh):
    placed = (P("leaf", "col", None), P(), P("leaf", "col"))
    return jax.shard_map(
        per_device,
        mesh=mesh,
        in_specs=placed,
        out_specs=(P("leaf", "col", None), P("leaf", "col")),
        check_vma=False,
    )
```
